512 devices in a mesh: seq: 64 (over y, z_lo, core), head: 8 (over z_hi, x).
Axes of the slice: x: 4, y: 4, z: 16 (z_hi: 2, z_lo: 8; z = z_hi * 8 + z_lo), core: 2. Of those that a mesh axis runs over, the one named last changes fastest.
Arguments:
- queries: bfloat16 [16384, 32, 128], P('seq', 'head'), may hold values from -48 to 48
- keys: bfloat16 [16384, 32, 128], P('seq', 'head'), may hold values from -6 to 6
- values: bfloat16 [16384, 32, 128], P('seq', 'head'), may hold values from -6 to 6
- attended: bfloat16 [16384, 32, 128], P('seq', 'head'), may hold values from -6 to 6
- out_grads: bfloat16 [16384, 32, 128], P('seq', 'head'), may hold values from -6 to 6
Outputs:
- grad_queries: bfloat16 [16384, 32, 128], P(('seq', 'head'))
- grad_keys: bfloat16 [16384, 32, 128], P(('seq', 'head'))
- grad_values: bfloat16 [16384, 32, 128], P(('seq', 'head'))
The draws below stay inside these ranges and needn't reach their ends.
All inputs are finite; a program needn't handle non-finite values.
Results may differ from the reference program's by a relative error of at most 0.005.
Values may be sent and summed in bfloat16 or wider, within the bound.
A program may use at most 64 MiB of HBM per device.

```python
import jax
import jax.numpy as jnp
from jax import lax

TOK_DEV = 256
SPAN = 4
HEADS = 32
HD = 128
TOKENS = 16384


def draw_keys(key, part):
    key = jax.random.fold_in(key, 5)
    return jnp.clip(jax.random.normal(key, (TOKENS, HEADS, HD), jnp.float32), -6.0, 6.0).astype(jnp.bfloat16)


def draw_queries(key, part):
    key = jax.random.fold_in(key, 7)
    return jnp.clip(jax.random.normal(key, (TOKENS, HEADS, HD), jnp.float32), -6.0, 6.0).astype(jnp.bfloat16)


def block_scale(key, dims, split, low, high):
    level = 1.0
    for dim, parts in split:
        steps = jax.random.uniform(jax.random.fold_in(jax.random.fold_in(key, 6), dim), (parts,), jnp.float32, low / len(split), high / len(split))
        level = level * jnp.repeat(jnp.exp(steps), dims[dim] // parts).reshape((-1,) + (1,) * (len(dims) - 1 - dim))
    return level


def gaussian(rng, extent, scale, bound, cuts=(), held_as=jnp.bfloat16):
    loudness = block_scale(rng, extent, cuts, -0.22, 0.18) if cuts else 1.0
    values = jax.random.normal(rng, extent, jnp.float32) * scale * loudness
    return jnp.minimum(jnp.maximum(values, -bound), bound).astype(held_as)


def setup_inputs(seed: int = 0) -> dict:
    key_list = jax.random.split(jax.random.key(seed), 6)
    queries = draw_queries(jax.random.fold_in(key_list[5], 71), 0)
    keys = draw_keys(jax.random.fold_in(key_list[5], 71), 0)
    values = gaussian(key_list[2], (TOKENS, HEADS, HD), 1.0, 6.0, ((0, 64), (1, 8)))
    attended = gaussian(key_list[3], (TOKENS, HEADS, HD), 1.0, 6.0, ((0, 64), (1, 8)))
    out_grads = gaussian(key_list[4], (TOKENS, HEADS, HD), 1.0, 6.0, ((0, 64), (1, 8)))
    return {"queries": queries, "keys": keys, "values": values, "attended": attended, "out_grads": out_grads}


def block_grads(query_rows, key_rows, value_rows, output_rows, grad_rows):
    scaling = HD ** -0.5
    scores = jnp.dot(query_rows, key_rows.T, preferred_element_type=jnp.float32) * scaling
    length = scores.shape[0]
    allowed = jnp.arange(length)[None, :] <= jnp.arange(length)[:, None]
    scores = jnp.where(allowed, scores, -jnp.inf)
    highest = jnp.max(scores, axis=1, keepdims=True)
    log_total = highest + jnp.log(jnp.sum(jnp.exp(scores - highest), axis=1, keepdims=True))
    weights = jnp.exp(scores - log_total)
    correction = jnp.sum(grad_rows.astype(jnp.float32) * output_rows.astype(jnp.float32), axis=1, keepdims=True)
    weights_low = weights.astype(jnp.bfloat16)
    grad_value = jnp.dot(weights_low.T, grad_rows, preferred_element_type=jnp.float32)
    grad_weights = jnp.dot(grad_rows, value_rows.T, preferred_element_type=jnp.float32)
    grad_scores = (weights * (grad_weights - correction) * scaling).astype(jnp.bfloat16)
    grad_query = jnp.dot(grad_scores, key_rows, preferred_element_type=jnp.float32)
    grad_key = jnp.dot(grad_scores.T, query_rows, preferred_element_type=jnp.float32)
    return (grad_query.astype(jnp.bfloat16), grad_key.astype(jnp.bfloat16), grad_value.astype(jnp.bfloat16))


def reference(queries, keys, values, attended, out_grads):
    block_len = SPAN * TOK_DEV
    block_count = TOKENS // block_len

    def arrange(array):
        return array.reshape(block_count, block_len, HEADS, HD).transpose(0, 2, 1, 3)

    def one_head(items):
        return block_grads(items[0], items[1], items[2], items[3], items[4])

    def one_block(items):
        return lax.map(one_head, items)

    arranged = (arrange(queries), arrange(keys), arrange(values), arrange(attended), arrange(out_grads))
    results = lax.map(one_block, arranged)

    def restore(array):
        return array.transpose(0, 2, 1, 3).reshape(TOKENS, HEADS, HD)

    return (restore(results[0]), restore(results[1]), restore(results[2]))
```

```python
import functools

import jax
import jax.numpy as jnp
from jax import lax
from jax.experimental import pallas as pl
from jax.experimental.pallas import tpu as pltpu
from jax.sharding import PartitionSpec as P

MESH = pl.DeviceIdType.MESH
BF16 = jnp.bfloat16
F32 = jnp.float32
SPAN = 4
TOK = 256
HL = 4
HD = 128
LEN = SPAN * TOK
HEADS = 32
PEERS = 32
ROWS = 32
SCALE = HD**-0.5

NT = (((1,), (1,)), ((), ()))


def dot(a, b):
    return jnp.dot(a, b, preferred_element_type=F32)


def dot_nt(a, b):
    return lax.dot_general(a, b, NT, preferred_element_type=F32)


def kernel(
    q_ref, k_ref, v_ref, o_ref, g_ref,
    dq_out, dk_out, dv_out,
    wide, send_in, send_corr, local_o, full, corr, grads, landed,
    in_send, in_recv, c_send, c_recv, out_send, out_recv, own_sem,
):
    seq = lax.axis_index("seq")
    head = lax.axis_index("head")
    base = (seq // SPAN) * SPAN
    place = seq % SPAN
    zh, x = head // 4, head % 4

    def peer(m):
        d_head, d_place = m // SPAN, m % SPAN
        to_zh = (zh + d_head // 4) % 2
        to_x = (x + d_head % 4) % 4
        to_place = (place + d_place) % SPAN
        return to_zh * 4 + to_x, to_place

    def source(m):
        d_head, d_place = m // SPAN, m % SPAN
        from_zh = (zh + d_head // 4) % 2
        from_x = (x + 4 - d_head % 4) % 4
        from_place = (place + SPAN - d_place) % SPAN
        return from_zh * 4 + from_x, from_place

    barrier = pltpu.get_barrier_semaphore()

    def greet(m, carry):
        to_head, to_place = source(m)
        pl.semaphore_signal(
            barrier, inc=1, device_id=(base + to_place, to_head), device_id_type=MESH
        )
        return carry

    lax.fori_loop(1, PEERS, greet, 0)

    def split_heads(ref, store):
        wide[...] = ref[...].astype(F32)
        for h in range(HL):
            store(h, wide[pl.ds(h, TOK, HL), :].astype(BF16))

    def store_in(a):
        def store(h, rows):
            send_in[a, h] = rows

        return store

    def store_o(h, rows):
        local_o[h] = rows

    def in_copy(a, d):
        to_place = (place + d) % SPAN
        return pltpu.make_async_remote_copy(
            src_ref=send_in.at[a, to_place],
            dst_ref=full.at[a, place],
            send_sem=in_send.at[a, d],
            recv_sem=in_recv.at[a, d],
            device_id=(base + to_place, head),
            device_id_type=MESH,
        )

    def corr_copy(d):
        to_place = (place + d) % SPAN
        return pltpu.make_async_remote_copy(
            src_ref=send_corr.at[to_place],
            dst_ref=corr.at[place],
            send_sem=c_send.at[d],
            recv_sem=c_recv.at[d],
            device_id=(base + to_place, head),
            device_id_type=MESH,
        )

    refs = (k_ref, q_ref, g_ref, v_ref)
    order = (2, 1, 3)
    split_heads(refs[0], store_in(0))
    pl.semaphore_wait(barrier, PEERS - 1)
    for a in range(4):
        if a:
            split_heads(refs[a], store_in(a))
        for d in order:
            in_copy(a, d).start()
    split_heads(o_ref, store_o)
    ones = jnp.ones((8, HD), BF16)
    for h in range(HL):
        prod = send_in[2, h].astype(F32) * local_o[h].astype(F32)
        high = prod.astype(BF16)
        low = (prod - high.astype(F32)).astype(BF16)
        send_corr[h] = dot_nt(ones, high) + dot_nt(ones, low)
    for d in order:
        corr_copy(d).start()
    for a in range(4):
        full[a, place] = send_in[a, place]
    corr[place] = send_corr[place]
    for a in range(4):
        for d in order:
            in_copy(a, d).wait()
    for d in order:
        corr_copy(d).wait()

    keys_t = full[0].reshape(LEN, HD).T
    row = lax.broadcasted_iota(jnp.int32, (TOK, TOK), 0)
    col = lax.broadcasted_iota(jnp.int32, (TOK, TOK), 1)
    dk_acc = [jnp.zeros((TOK, HD), F32) for _ in range(SPAN)]
    dv_acc = [jnp.zeros((TOK, HD), F32) for _ in range(SPAN)]
    for i in range(SPAN):
        q = full[1, i]
        g = full[2, i]
        c = corr[i][0:1, :]
        scores = []
        for j in range(i + 1):
            s = dot_nt(full[0, j], q) * SCALE
            if i == j:
                s = jnp.where(row <= col, s, -jnp.inf)
            scores.append(s)
        top = jnp.max(scores[0], axis=0, keepdims=True)
        for s in scores[1:]:
            top = jnp.maximum(top, jnp.max(s, axis=0, keepdims=True))
        exps = [jnp.exp(s - top) for s in scores]
        total = jnp.sum(exps[0], axis=0, keepdims=True)
        for e in exps[1:]:
            total = total + jnp.sum(e, axis=0, keepdims=True)
        inv = 1.0 / total
        dq_t = jnp.zeros((HD, TOK), F32)
        for j in range(i + 1):
            w = exps[j] * inv
            dv_acc[j] = dv_acc[j] + dot(w.astype(BF16), g)
            gw = dot_nt(full[3, j], g)
            ds = (w * (gw - c)).astype(BF16)
            dk_acc[j] = dk_acc[j] + dot(ds, q)
            dq_t = dq_t + dot(keys_t[:, j * TOK : (j + 1) * TOK], ds)
        grads[0, i] = (dq_t * SCALE).T.astype(BF16)
    for j in range(SPAN):
        grads[1, j] = (dk_acc[j] * SCALE).astype(BF16)
        grads[2, j] = dv_acc[j].astype(BF16)

    mine = head * HL + place

    def out_copy(m):
        to_head, to_place = peer(m)
        return pltpu.make_async_remote_copy(
            src_ref=grads.at[:, to_place, pl.ds(pl.multiple_of(to_head * ROWS, ROWS), ROWS)],
            dst_ref=landed.at[:, mine],
            send_sem=out_send.at[m],
            recv_sem=out_recv.at[m],
            device_id=(base + to_place, to_head),
            device_id_type=MESH,
        )

    def send(t, carry):
        out_copy(PEERS - 1 - t).start()
        return carry

    def wait(t, carry):
        out_copy(PEERS - 1 - t).wait()
        return carry

    lax.fori_loop(0, PEERS - 1, send, 0)
    own = pltpu.make_async_copy(
        grads.at[:, place, pl.ds(pl.multiple_of(head * ROWS, ROWS), ROWS)],
        landed.at[:, mine],
        own_sem,
    )
    own.start()
    own.wait()
    lax.fori_loop(0, PEERS - 1, wait, 0)

    for a, out in enumerate((dq_out, dk_out, dv_out)):
        wide[...] = landed[a].reshape(HEADS * ROWS, HD).astype(F32)
        for t in range(ROWS):
            out[t] = wide[pl.ds(t, HEADS, ROWS), :].astype(BF16)


def body(q, k, v, o, g):
    flat = [z.reshape(TOK * HL, HD) for z in (q, k, v, o, g)]
    vmem = pl.BlockSpec(memory_space=pltpu.VMEM)
    return pl.pallas_call(
        kernel,
        out_shape=[jax.ShapeDtypeStruct((ROWS, HEADS, HD), BF16)] * 3,
        in_specs=[vmem] * 5,
        out_specs=[vmem] * 3,
        scratch_shapes=[
            pltpu.VMEM((TOK * HL, HD), F32),
            pltpu.VMEM((4, HL, TOK, HD), BF16),
            pltpu.VMEM((HL, 8, TOK), F32),
            pltpu.VMEM((HL, TOK, HD), BF16),
            pltpu.VMEM((4, SPAN, TOK, HD), BF16),
            pltpu.VMEM((SPAN, 8, TOK), F32),
            pltpu.VMEM((3, SPAN, TOK, HD), BF16),
            pltpu.VMEM((3, HEADS, ROWS, HD), BF16),
            pltpu.SemaphoreType.DMA((4, SPAN)),
            pltpu.SemaphoreType.DMA((4, SPAN)),
            pltpu.SemaphoreType.DMA((SPAN,)),
            pltpu.SemaphoreType.DMA((SPAN,)),
            pltpu.SemaphoreType.DMA((PEERS,)),
            pltpu.SemaphoreType.DMA((PEERS,)),
            pltpu.SemaphoreType.DMA,
        ],
        compiler_params=pltpu.CompilerParams(
            collective_id=0, has_side_effects=True, vmem_limit_bytes=40 * 1024 * 1024
        ),
        name="grads",
    )(*flat)


def solution(mesh):
    placed = P("seq", "head", None)
    gathered = P(("seq", "head"), None, None)
    return jax.shard_map(
        body,
        mesh=mesh,
        in_specs=(placed,) * 5,
        out_specs=(gathered,) * 3,
        check_vma=False,
    )
```

```python
import functools

import jax
import jax.numpy as jnp
from jax import lax
from jax.experimental import pallas as pl
from jax.experimental.pallas import tpu as pltpu
from jax.sharding import PartitionSpec as P

MESH = pl.DeviceIdType.MESH
BF16 = jnp.bfloat16
F32 = jnp.float32
SPAN = 4
TOK = 256
HL = 4
HD = 128
HEADS = 32
PEERS = 32
ROWS = 32
SCALE = HD**-0.5
K, Q, G, V = range(4)

NT = (((1,), (1,)), ((), ()))


def dot(a, b):
    return jnp.dot(a, b, preferred_element_type=F32)


def dot_nt(a, b):
    return lax.dot_general(a, b, NT, preferred_element_type=F32)


def kernel(
    k_hbm, q_hbm, g_hbm, v_hbm, o_hbm,
    landed,
    stage, wide, send_in, send_corr, local_o, full, keys_t, corr, acc, grads,
    hbm_sem, in_send, in_recv, c_send, c_recv, out_send, out_recv, own_sem,
):
    seq = lax.axis_index("seq")
    head = lax.axis_index("head")
    base = (seq // SPAN) * SPAN
    place = seq % SPAN
    mine = head * HL + place

    def shifted(h, d):
        return ((h // 4 + d // 4) % 2) * 4 + (h % 4 + d % 4) % 4

    def back(h, d):
        return ((h // 4 + d // 4) % 2) * 4 + (h % 4 + 4 - d % 4) % 4

    loads = []
    for a, ref in enumerate((k_hbm, q_hbm, g_hbm, v_hbm, o_hbm)):
        loads.append(pltpu.make_async_copy(ref, stage.at[a], hbm_sem.at[a]))
        loads[-1].start()

    barrier = pltpu.get_barrier_semaphore()

    def greet(m, carry):
        to = (base + (place + SPAN - m % SPAN) % SPAN, back(head, m // SPAN))
        pl.semaphore_signal(barrier, inc=1, device_id=to, device_id_type=MESH)
        return carry

    lax.fori_loop(1, PEERS, greet, 0)

    def split_heads(a, store):
        loads[a].wait()
        wide[...] = stage[a].astype(F32)
        for h in range(HL):
            store(h, wide[pl.ds(h, TOK, HL), :].astype(BF16))

    def store_in(a):
        def store(h, rows):
            send_in[a, h] = rows

        return store

    def store_o(h, rows):
        local_o[h] = rows

    same_chip = place + 1 - 2 * (place % 2)
    others = (same_chip, (place + 2) % SPAN, (same_chip + 2) % SPAN)

    def in_copy(a, r):
        return pltpu.make_async_remote_copy(
            src_ref=send_in.at[a, others[r]],
            dst_ref=full.at[a, place],
            send_sem=in_send.at[a, r],
            recv_sem=in_recv.at[a, r],
            device_id=(base + others[r], head),
            device_id_type=MESH,
        )

    def corr_copy(r):
        return pltpu.make_async_remote_copy(
            src_ref=send_corr.at[others[r]],
            dst_ref=corr.at[place],
            send_sem=c_send.at[r],
            recv_sem=c_recv.at[r],
            device_id=(base + others[r], head),
            device_id_type=MESH,
        )

    split_heads(K, store_in(K))
    pl.semaphore_wait(barrier, PEERS - 1)
    for r in (1, 2, 0):
        in_copy(K, r).start()
    split_heads(V, store_in(V))

    @pl.when(place < 2)
    def _():
        for r in (1, 2, 0):
            in_copy(V, r).start()

    for a in (Q, G):
        split_heads(a, store_in(a))
        for r in (1, 2, 0):
            in_copy(a, r).start()

    @pl.when(place >= 2)
    def _():
        for r in (0, 1, 2):
            in_copy(V, r).start()

    split_heads(4, store_o)
    ones = jnp.ones((8, HD), BF16)
    for h in range(HL):
        prod = send_in[G, h].astype(F32) * local_o[h].astype(F32)
        high = prod.astype(BF16)
        low = (prod - high.astype(F32)).astype(BF16)
        send_corr[h] = dot_nt(ones, high) + dot_nt(ones, low)
    for r in (0, 1, 2):
        corr_copy(r).start()
    for a in range(4):
        full[a, place] = send_in[a, place]
    corr[place] = send_corr[place]

    def rows(i, first):
        q = full[Q, i]
        g = full[G, i]
        c = corr[i][0:1, :]
        row = lax.broadcasted_iota(jnp.int32, (TOK, TOK), 0)
        col = lax.broadcasted_iota(jnp.int32, (TOK, TOK), 1)
        scores = []
        for j in range(i + 1):
            s = dot_nt(full[K, j], q) * SCALE
            if i == j:
                s = jnp.where(row <= col, s, -jnp.inf)
            scores.append(s)
        top = jnp.max(scores[0], axis=0, keepdims=True)
        for s in scores[1:]:
            top = jnp.maximum(top, jnp.max(s, axis=0, keepdims=True))
        exps = [jnp.exp(s - top) for s in scores]
        total = jnp.sum(exps[0], axis=0, keepdims=True)
        for e in exps[1:]:
            total = total + jnp.sum(e, axis=0, keepdims=True)
        inv = 1.0 / total
        dq_t = jnp.zeros((HD, TOK), F32)
        for j in range(i + 1):
            w = exps[j] * inv
            dv = dot(w.astype(BF16), g)
            gw = dot_nt(full[V, j], g)
            ds = (w * (gw - c)).astype(BF16)
            dk = dot(ds, q)
            if j in first:
                acc[0, j] = acc[0, j] + dk
                acc[1, j] = acc[1, j] + dv
            else:
                acc[0, j] = dk
                acc[1, j] = dv
                first.add(j)
            dq_t = dq_t + dot(keys_t[j], ds)
        grads[0, i] = (dq_t * SCALE).T.astype(BF16)

    def finish(j):
        grads[1, j] = (acc[0, j] * SCALE).astype(BF16)
        grads[2, j] = acc[1, j].astype(BF16)

    def out_copy(a0, a1, p, d):
        to_head = shifted(head, d)
        m = d * SPAN + (p + SPAN - place) % SPAN
        return pltpu.make_async_remote_copy(
            src_ref=grads.at[a0:a1, p, pl.ds(pl.multiple_of(to_head * ROWS, ROWS), ROWS)],
            dst_ref=landed.at[a0:a1, mine],
            send_sem=out_send.at[m],
            recv_sem=out_recv.at[m],
            device_id=(base + p, to_head),
            device_id_type=MESH,
        )

    def own_copy(a0, a1):
        return pltpu.make_async_copy(
            grads.at[a0:a1, place, pl.ds(pl.multiple_of(head * ROWS, ROWS), ROWS)],
            landed.at[a0:a1, mine],
            own_sem,
        )

    def send(a0, a1, p0):
        def step(t, carry):
            d = (4 + t // 2) % 8
            p = p0 + t % 2
            me = jnp.logical_and(d == 0, p == place)

            @pl.when(me)
            def _():
                own_copy(a0, a1).start()

            @pl.when(jnp.logical_not(me))
            def _():
                out_copy(a0, a1, p, d).start()

            return carry

        lax.fori_loop(0, 16, step, 0)

    def turn(j):
        keys_t[j] = full[K, j].T

    for a in range(4):
        in_copy(a, 0).wait_recv()
    corr_copy(0).wait_recv()

    @pl.when(place < 2)
    def _():
        first = set()
        for i in (0, 1):
            turn(i)
            rows(i, first)
        send(0, 1, 0)
        for a in (K, Q, G, V):
            for r in (1, 2):
                in_copy(a, r).wait_recv()
        for r in (1, 2):
            corr_copy(r).wait_recv()
        turn(2)
        turn(3)
        rows(3, first)
        rows(2, first)
        for j in range(SPAN):
            finish(j)
        send(0, 3, 2)
        send(1, 3, 0)

    @pl.when(place >= 2)
    def _():
        first = set()
        turn(2)
        turn(3)
        for a in (K, V):
            for r in (1, 2):
                in_copy(a, r).wait_recv()
        turn(0)
        turn(1)
        rows(2, first)
        rows(3, first)
        finish(2)
        finish(3)
        send(0, 3, 2)
        for a in (Q, G):
            for r in (1, 2):
                in_copy(a, r).wait_recv()
        for r in (1, 2):
            corr_copy(r).wait_recv()
        rows(1, first)
        rows(0, first)
        finish(0)
        finish(1)
        send(0, 3, 0)

    for a in range(4):
        for r in range(3):
            in_copy(a, r).wait_send()
    for r in range(3):
        corr_copy(r).wait_send()
    own_copy(0, 3).wait()

    def wait(m, carry):
        out_copy(0, 3, (place + m) % SPAN, m // SPAN).wait()
        return carry

    lax.fori_loop(1, PEERS, wait, 0)


def arrange(landed_hbm, dq_out, dk_out, dv_out, landed, wide, done, in_sem, sem):
    loads = [
        pltpu.make_async_copy(landed_hbm.at[a], landed.at[a], in_sem.at[a]) for a in range(3)
    ]
    for load in loads:
        load.start()
    copies = []
    for a, out in enumerate((dq_out, dk_out, dv_out)):
        loads[a].wait()
        wide[a] = landed[a].reshape(HEADS * ROWS, HD).astype(F32)
        for t in range(ROWS):
            done[a, t] = wide[a, pl.ds(t, HEADS, ROWS), :].astype(BF16)
        copies.append(pltpu.make_async_copy(done.at[a], out, sem.at[a]))
        copies[-1].start()
    for copy in copies:
        copy.wait()


def body(q, k, v, o, g):
    flat = [z.reshape(TOK * HL, HD) for z in (k, q, g, v, o)]
    hbm = pl.BlockSpec(memory_space=pltpu.HBM)
    landed = pl.pallas_call(
        kernel,
        out_shape=jax.ShapeDtypeStruct((3, HEADS, ROWS, HD), BF16),
        in_specs=[hbm] * 5,
        out_specs=hbm,
        scratch_shapes=[
            pltpu.VMEM((5, TOK * HL, HD), BF16),
            pltpu.VMEM((TOK * HL, HD), F32),
            pltpu.VMEM((4, HL, TOK, HD), BF16),
            pltpu.VMEM((HL, 8, TOK), F32),
            pltpu.VMEM((HL, TOK, HD), BF16),
            pltpu.VMEM((4, SPAN, TOK, HD), BF16),
            pltpu.VMEM((SPAN, HD, TOK), BF16),
            pltpu.VMEM((SPAN, 8, TOK), F32),
            pltpu.VMEM((2, SPAN, TOK, HD), F32),
            pltpu.VMEM((3, SPAN, TOK, HD), BF16),
            pltpu.SemaphoreType.DMA((5,)),
            pltpu.SemaphoreType.DMA((4, 3)),
            pltpu.SemaphoreType.DMA((4, 3)),
            pltpu.SemaphoreType.DMA((3,)),
            pltpu.SemaphoreType.DMA((3,)),
            pltpu.SemaphoreType.DMA((PEERS,)),
            pltpu.SemaphoreType.DMA((PEERS,)),
            pltpu.SemaphoreType.DMA,
        ],
        compiler_params=pltpu.CompilerParams(
            collective_id=0, has_side_effects=True, vmem_limit_bytes=60 * 1024 * 1024
        ),
        name="grads",
    )(*flat)
    return pl.pallas_call(
        arrange,
        out_shape=[jax.ShapeDtypeStruct((ROWS, HEADS, HD), BF16)] * 3,
        in_specs=[hbm],
        out_specs=[hbm] * 3,
        scratch_shapes=[
            pltpu.VMEM((3, HEADS, ROWS, HD), BF16),
            pltpu.VMEM((3, HEADS * ROWS, HD), F32),
            pltpu.VMEM((3, ROWS, HEADS, HD), BF16),
            pltpu.SemaphoreType.DMA((3,)),
            pltpu.SemaphoreType.DMA((3,)),
        ],
        compiler_params=pltpu.CompilerParams(vmem_limit_bytes=60 * 1024 * 1024),
        name="arrange",
    )(landed)


def solution(mesh):
    placed = P("seq", "head", None)
    gathered = P(("seq", "head"), None, None)
    return jax.shard_map(
        body,
        mesh=mesh,
        in_specs=(placed,) * 5,
        out_specs=(gathered,) * 3,
        check_vma=False,
    )
```

```python
import functools

import jax
import jax.numpy as jnp
from jax import lax
from jax.experimental import pallas as pl
from jax.experimental.pallas import tpu as pltpu
from jax.sharding import PartitionSpec as P

MESH = pl.DeviceIdType.MESH
BF16 = jnp.bfloat16
F32 = jnp.float32
SPAN = 4
TOK = 256
HL = 4
HD = 128
HEADS = 32
PEERS = 32
NEAR = 16
ROWS = 32
SCALE = HD**-0.5
K, Q, G, V = range(4)

NT = (((1,), (1,)), ((), ()))


def dot(a, b):
    return jnp.dot(a, b, preferred_element_type=F32)


def dot_nt(a, b):
    return lax.dot_general(a, b, NT, preferred_element_type=F32)


def kernel(
    k_hbm, q_hbm, g_hbm, v_hbm, o_hbm,
    landed,
    stage, wide, send_in, send_corr, local_o, full, keys_t, corr, acc, grads,
    hbm_sem, in_send, in_recv, c_send, c_recv, out_send, out_recv, own_sem,
):
    seq = lax.axis_index("seq")
    head = lax.axis_index("head")
    base = (seq // SPAN) * SPAN
    place = seq % SPAN
    mine = head * HL + place

    def shifted(h, d):
        return ((h // 4 + d // 4) % 2) * 4 + (h % 4 + d % 4) % 4

    def back(h, d):
        return ((h // 4 + d // 4) % 2) * 4 + (h % 4 + 4 - d % 4) % 4

    loads = []
    for a, ref in enumerate((k_hbm, q_hbm, g_hbm, v_hbm, o_hbm)):
        loads.append(pltpu.make_async_copy(ref, stage.at[a], hbm_sem.at[a]))
        loads[-1].start()

    barrier = pltpu.get_barrier_semaphore()

    def greet(m, carry):
        to = (base + (place + SPAN - m % SPAN) % SPAN, back(head, m // SPAN))
        pl.semaphore_signal(barrier, inc=1, device_id=to, device_id_type=MESH)
        return carry

    lax.fori_loop(1, NEAR, greet, 0)
    upper = head >= 4

    def split_heads(a, store):
        loads[a].wait()
        wide[...] = stage[a].astype(F32)
        for h in range(HL):
            store(h, wide[pl.ds(h, TOK, HL), :].astype(BF16))

    def store_in(a):
        def store(h, rows):
            send_in[a, h] = rows

        return store

    def store_o(h, rows):
        local_o[h] = rows

    same_chip = place + 1 - 2 * (place % 2)
    others = (same_chip, (place + 2) % SPAN, (same_chip + 2) % SPAN)

    def in_copy(a, r):
        return pltpu.make_async_remote_copy(
            src_ref=send_in.at[a, others[r]],
            dst_ref=full.at[a, place],
            send_sem=in_send.at[a, r],
            recv_sem=in_recv.at[a, r],
            device_id=(base + others[r], head),
            device_id_type=MESH,
        )

    def corr_copy(r):
        return pltpu.make_async_remote_copy(
            src_ref=send_corr.at[others[r]],
            dst_ref=corr.at[place],
            send_sem=c_send.at[r],
            recv_sem=c_recv.at[r],
            device_id=(base + others[r], head),
            device_id_type=MESH,
        )

    split_heads(K, store_in(K))
    @pl.when(upper)
    def _():
        pl.semaphore_wait(barrier, PEERS - 1)

    @pl.when(jnp.logical_not(upper))
    def _():
        pl.semaphore_wait(barrier, NEAR - 1)

    lax.fori_loop(NEAR, PEERS, greet, 0)
    for r in (1, 2, 0):
        in_copy(K, r).start()
    split_heads(V, store_in(V))

    @pl.when(place < 2)
    def _():
        for r in (1, 2, 0):
            in_copy(V, r).start()

    for a in (Q, G):
        split_heads(a, store_in(a))
        for r in (1, 2, 0):
            in_copy(a, r).start()

    @pl.when(place >= 2)
    def _():
        for r in (0, 1, 2):
            in_copy(V, r).start()

    split_heads(4, store_o)
    ones = jnp.ones((8, HD), BF16)
    for h in range(HL):
        prod = send_in[G, h].astype(F32) * local_o[h].astype(F32)
        high = prod.astype(BF16)
        low = (prod - high.astype(F32)).astype(BF16)
        send_corr[h] = dot_nt(ones, high) + dot_nt(ones, low)
    for r in (0, 1, 2):
        corr_copy(r).start()
    for a in range(4):
        full[a, place] = send_in[a, place]
    corr[place] = send_corr[place]

    def rows(i, first):
        q = full[Q, i]
        g = full[G, i]
        c = corr[i][0:1, :]
        row = lax.broadcasted_iota(jnp.int32, (TOK, TOK), 0)
        col = lax.broadcasted_iota(jnp.int32, (TOK, TOK), 1)
        scores = []
        for j in range(i + 1):
            s = dot_nt(full[K, j], q) * SCALE
            if i == j:
                s = jnp.where(row <= col, s, -jnp.inf)
            scores.append(s)
        top = jnp.max(scores[0], axis=0, keepdims=True)
        for s in scores[1:]:
            top = jnp.maximum(top, jnp.max(s, axis=0, keepdims=True))
        exps = [jnp.exp(s - top) for s in scores]
        total = jnp.sum(exps[0], axis=0, keepdims=True)
        for e in exps[1:]:
            total = total + jnp.sum(e, axis=0, keepdims=True)
        inv = 1.0 / total
        dq_t = jnp.zeros((HD, TOK), F32)
        for j in range(i + 1):
            w = exps[j] * inv
            dv = dot(w.astype(BF16), g)
            gw = dot_nt(full[V, j], g)
            ds = (w * (gw - c)).astype(BF16)
            dk = dot(ds, q)
            if j in first:
                acc[0, j] = acc[0, j] + dk
                acc[1, j] = acc[1, j] + dv
            else:
                acc[0, j] = dk
                acc[1, j] = dv
                first.add(j)
            dq_t = dq_t + dot(keys_t[j], ds)
        grads[0, i] = (dq_t * SCALE).T.astype(BF16)

    def finish(j):
        grads[1, j] = (acc[0, j] * SCALE).astype(BF16)
        grads[2, j] = acc[1, j].astype(BF16)

    def out_copy(a0, a1, p, d):
        to_head = shifted(head, d)
        m = d * SPAN + (p + SPAN - place) % SPAN
        return pltpu.make_async_remote_copy(
            src_ref=grads.at[a0:a1, p, pl.ds(pl.multiple_of(to_head * ROWS, ROWS), ROWS)],
            dst_ref=landed.at[a0:a1, mine],
            send_sem=out_send.at[m],
            recv_sem=out_recv.at[m],
            device_id=(base + p, to_head),
            device_id_type=MESH,
        )

    def own_copy(a0, a1):
        return pltpu.make_async_copy(
            grads.at[a0:a1, place, pl.ds(pl.multiple_of(head * ROWS, ROWS), ROWS)],
            landed.at[a0:a1, mine],
            own_sem,
        )

    def send_half(a0, a1, p0, d0):
        def step(t, carry):
            d = d0 + t // 2
            p = p0 + t % 2
            me = jnp.logical_and(d == 0, p == place)

            @pl.when(me)
            def _():
                own_copy(a0, a1).start()

            @pl.when(jnp.logical_not(me))
            def _():
                out_copy(a0, a1, p, d).start()

            return carry

        lax.fori_loop(0, 8, step, 0)

    def send(a0, a1, p0):
        @pl.when(upper)
        def _():
            send_half(a0, a1, p0, 4)

        send_half(a0, a1, p0, 0)

    def turn(j):
        keys_t[j] = full[K, j].T

    for a in range(4):
        in_copy(a, 0).wait_recv()
    corr_copy(0).wait_recv()

    @pl.when(place < 2)
    def _():
        first = set()
        for i in (0, 1):
            turn(i)
            rows(i, first)
        send(0, 1, 0)
        for a in (K, Q, G, V):
            for r in (1, 2):
                in_copy(a, r).wait_recv()
        for r in (1, 2):
            corr_copy(r).wait_recv()
        turn(2)
        turn(3)
        rows(3, first)
        rows(2, first)
        for j in range(SPAN):
            finish(j)
        send(0, 3, 2)
        send(1, 3, 0)

    @pl.when(place >= 2)
    def _():
        first = set()
        turn(2)
        turn(3)
        for a in (K, V):
            for r in (1, 2):
                in_copy(a, r).wait_recv()
        turn(0)
        turn(1)
        rows(2, first)
        rows(3, first)
        finish(2)
        finish(3)
        send(0, 3, 2)
        for a in (Q, G):
            for r in (1, 2):
                in_copy(a, r).wait_recv()
        for r in (1, 2):
            corr_copy(r).wait_recv()
        rows(1, first)
        rows(0, first)
        finish(0)
        finish(1)
        send(0, 3, 0)

    @pl.when(jnp.logical_not(upper))
    def _():
        pl.semaphore_wait(barrier, PEERS - NEAR)
        send_half(0, 3, 2, 4)
        send_half(0, 3, 0, 4)

    for a in range(4):
        for r in range(3):
            in_copy(a, r).wait_send()
    for r in range(3):
        corr_copy(r).wait_send()
    own_copy(0, 3).wait()

    def wait(m, carry):
        out_copy(0, 3, (place + m) % SPAN, m // SPAN).wait()
        return carry

    lax.fori_loop(1, PEERS, wait, 0)


def arrange(landed_hbm, dq_out, dk_out, dv_out, landed, wide, done, in_sem, sem):
    loads = [
        pltpu.make_async_copy(landed_hbm.at[a], landed.at[a], in_sem.at[a]) for a in range(3)
    ]
    for load in loads:
        load.start()
    copies = []
    for a, out in enumerate((dq_out, dk_out, dv_out)):
        loads[a].wait()
        wide[a] = landed[a].reshape(HEADS * ROWS, HD).astype(F32)
        for t in range(ROWS):
            done[a, t] = wide[a, pl.ds(t, HEADS, ROWS), :].astype(BF16)
        copies.append(pltpu.make_async_copy(done.at[a], out, sem.at[a]))
        copies[-1].start()
    for copy in copies:
        copy.wait()


def body(q, k, v, o, g):
    flat = [z.reshape(TOK * HL, HD) for z in (k, q, g, v, o)]
    hbm = pl.BlockSpec(memory_space=pltpu.HBM)
    landed = pl.pallas_call(
        kernel,
        out_shape=jax.ShapeDtypeStruct((3, HEADS, ROWS, HD), BF16),
        in_specs=[hbm] * 5,
        out_specs=hbm,
        scratch_shapes=[
            pltpu.VMEM((5, TOK * HL, HD), BF16),
            pltpu.VMEM((TOK * HL, HD), F32),
            pltpu.VMEM((4, HL, TOK, HD), BF16),
            pltpu.VMEM((HL, 8, TOK), F32),
            pltpu.VMEM((HL, TOK, HD), BF16),
            pltpu.VMEM((4, SPAN, TOK, HD), BF16),
            pltpu.VMEM((SPAN, HD, TOK), BF16),
            pltpu.VMEM((SPAN, 8, TOK), F32),
            pltpu.VMEM((2, SPAN, TOK, HD), F32),
            pltpu.VMEM((3, SPAN, TOK, HD), BF16),
            pltpu.SemaphoreType.DMA((5,)),
            pltpu.SemaphoreType.DMA((4, 3)),
            pltpu.SemaphoreType.DMA((4, 3)),
            pltpu.SemaphoreType.DMA((3,)),
            pltpu.SemaphoreType.DMA((3,)),
            pltpu.SemaphoreType.DMA((PEERS,)),
            pltpu.SemaphoreType.DMA((PEERS,)),
            pltpu.SemaphoreType.DMA,
        ],
        compiler_params=pltpu.CompilerParams(
            collective_id=0, has_side_effects=True, vmem_limit_bytes=60 * 1024 * 1024
        ),
        name="grads",
    )(*flat)
    return pl.pallas_call(
        arrange,
        out_shape=[jax.ShapeDtypeStruct((ROWS, HEADS, HD), BF16)] * 3,
        in_specs=[hbm],
        out_specs=[hbm] * 3,
        scratch_shapes=[
            pltpu.VMEM((3, HEADS, ROWS, HD), BF16),
            pltpu.VMEM((3, HEADS * ROWS, HD), F32),
            pltpu.VMEM((3, ROWS, HEADS, HD), BF16),
            pltpu.SemaphoreType.DMA((3,)),
            pltpu.SemaphoreType.DMA((3,)),
        ],
        compiler_params=pltpu.CompilerParams(vmem_limit_bytes=60 * 1024 * 1024),
        name="arrange",
    )(landed)


def solution(mesh):
    placed = P("seq", "head", None)
    gathered = P(("seq", "head"), None, None)
    return jax.shard_map(
        body,
        mesh=mesh,
        in_specs=(placed,) * 5,
        out_specs=(gathered,) * 3,
        check_vma=False,
    )
```

```python
import functools

import jax
import jax.numpy as jnp
from jax import lax
from jax.experimental import pallas as pl
from jax.experimental.pallas import tpu as pltpu
from jax.sharding import PartitionSpec as P

MESH = pl.DeviceIdType.MESH
BF16 = jnp.bfloat16
F32 = jnp.float32
SPAN = 4
TOK = 256
HL = 4
HD = 128
HEADS = 32
PEERS = 32
NEAR = 16
ROWS = 32
SCALE = HD**-0.5
K, Q, G, V = range(4)

NT = (((1,), (1,)), ((), ()))


def dot(a, b):
    return jnp.dot(a, b, preferred_element_type=F32)


def dot_nt(a, b):
    return lax.dot_general(a, b, NT, preferred_element_type=F32)


def kernel(
    k_hbm, q_hbm, g_hbm, v_hbm, o_hbm,
    landed,
    stage, wide, send_in, send_corr, local_o, full, keys_t, corr, acc, grads,
    hbm_sem, in_send, in_recv, c_send, c_recv, out_send, out_recv, own_sem,
):
    seq = lax.axis_index("seq")
    head = lax.axis_index("head")
    base = (seq // SPAN) * SPAN
    place = seq % SPAN
    mine = head * HL + place

    def shifted(h, d):
        return ((h // 4 + d // 4) % 2) * 4 + (h % 4 + d % 4) % 4

    def back(h, d):
        return ((h // 4 + d // 4) % 2) * 4 + (h % 4 + 4 - d % 4) % 4

    loads = []
    for a, ref in enumerate((k_hbm, q_hbm, g_hbm, v_hbm, o_hbm)):
        loads.append(pltpu.make_async_copy(ref, stage.at[a], hbm_sem.at[a]))
        loads[-1].start()

    barrier = pltpu.get_barrier_semaphore()

    def greet(m, carry):
        to = (base + (place + SPAN - m % SPAN) % SPAN, back(head, m // SPAN))
        pl.semaphore_signal(barrier, inc=1, device_id=to, device_id_type=MESH)
        return carry


    lax.fori_loop(1, NEAR, greet, 0)
    upper = head >= 4

    def split_heads(a, store):
        loads[a].wait()
        wide[...] = stage[a].astype(F32)
        for h in range(HL):
            store(h, wide[pl.ds(h, TOK, HL), :].astype(BF16))

    def store_in(a):
        def store(h, rows):
            send_in[a, h] = rows

        return store

    def store_o(h, rows):
        local_o[h] = rows

    same_chip = place + 1 - 2 * (place % 2)
    others = (same_chip, (place + 2) % SPAN, (same_chip + 2) % SPAN)

    def in_copy(a, r):
        return pltpu.make_async_remote_copy(
            src_ref=send_in.at[a, others[r]],
            dst_ref=full.at[a, place],
            send_sem=in_send.at[a, r],
            recv_sem=in_recv.at[a, r],
            device_id=(base + others[r], head),
            device_id_type=MESH,
        )

    def corr_copy(r):
        return pltpu.make_async_remote_copy(
            src_ref=send_corr.at[others[r]],
            dst_ref=corr.at[place],
            send_sem=c_send.at[r],
            recv_sem=c_recv.at[r],
            device_id=(base + others[r], head),
            device_id_type=MESH,
        )

    split_heads(K, store_in(K))
    lax.fori_loop(NEAR, PEERS, greet, 0)
    pl.semaphore_wait(barrier, PEERS - 1)
    for r in (1, 2, 0):
        in_copy(K, r).start()
    split_heads(V, store_in(V))

    @pl.when(place < 2)
    def _():
        for r in (1, 2, 0):
            in_copy(V, r).start()

    for a in (Q, G):
        split_heads(a, store_in(a))
        for r in (1, 2, 0):
            in_copy(a, r).start()

    @pl.when(place >= 2)
    def _():
        for r in (0, 1, 2):
            in_copy(V, r).start()

    split_heads(4, store_o)
    ones = jnp.ones((8, HD), BF16)
    for h in range(HL):
        prod = send_in[G, h].astype(F32) * local_o[h].astype(F32)
        high = prod.astype(BF16)
        low = (prod - high.astype(F32)).astype(BF16)
        send_corr[h] = dot_nt(ones, high) + dot_nt(ones, low)
    for r in (0, 1, 2):
        corr_copy(r).start()
    for a in range(4):
        full[a, place] = send_in[a, place]
    corr[place] = send_corr[place]

    def rows(i, first):
        q = full[Q, i]
        g = full[G, i]
        c = corr[i][0:1, :]
        row = lax.broadcasted_iota(jnp.int32, (TOK, TOK), 0)
        col = lax.broadcasted_iota(jnp.int32, (TOK, TOK), 1)
        scores = []
        for j in range(i + 1):
            s = dot_nt(full[K, j], q) * SCALE
            if i == j:
                s = jnp.where(row <= col, s, -jnp.inf)
            scores.append(s)
        top = jnp.max(scores[0], axis=0, keepdims=True)
        for s in scores[1:]:
            top = jnp.maximum(top, jnp.max(s, axis=0, keepdims=True))
        exps = [jnp.exp(s - top) for s in scores]
        total = jnp.sum(exps[0], axis=0, keepdims=True)
        for e in exps[1:]:
            total = total + jnp.sum(e, axis=0, keepdims=True)
        inv = 1.0 / total
        dq_t = jnp.zeros((HD, TOK), F32)
        for j in range(i + 1):
            w = exps[j] * inv
            dv = dot(w.astype(BF16), g)
            gw = dot_nt(full[V, j], g)
            ds = (w * (gw - c)).astype(BF16)
            dk = dot(ds, q)
            if j in first:
                acc[0, j] = acc[0, j] + dk
                acc[1, j] = acc[1, j] + dv
            else:
                acc[0, j] = dk
                acc[1, j] = dv
                first.add(j)
            dq_t = dq_t + dot(keys_t[j], ds)
        grads[0, i] = (dq_t * SCALE).T.astype(BF16)

    def finish(j):
        grads[1, j] = (acc[0, j] * SCALE).astype(BF16)
        grads[2, j] = acc[1, j].astype(BF16)

    def out_copy(a0, a1, p, d):
        to_head = shifted(head, d)
        m = d * SPAN + (p + SPAN - place) % SPAN
        return pltpu.make_async_remote_copy(
            src_ref=grads.at[a0:a1, p, pl.ds(pl.multiple_of(to_head * ROWS, ROWS), ROWS)],
            dst_ref=landed.at[a0:a1, mine],
            send_sem=out_send.at[m],
            recv_sem=out_recv.at[m],
            device_id=(base + p, to_head),
            device_id_type=MESH,
        )

    def own_copy(a0, a1):
        return pltpu.make_async_copy(
            grads.at[a0:a1, place, pl.ds(pl.multiple_of(head * ROWS, ROWS), ROWS)],
            landed.at[a0:a1, mine],
            own_sem,
        )

    def send_half(parts, d0):
        def step(t, carry):
            d = d0 + t // 2
            for a0, a1, p0 in parts:
                p = p0 + t % 2
                me = jnp.logical_and(d == 0, p == place)

                @pl.when(me)
                def _():
                    own_copy(a0, a1).start()

                @pl.when(jnp.logical_not(me))
                def _():
                    out_copy(a0, a1, p, d).start()

            return carry

        lax.fori_loop(0, 8, step, 0)

    def send(*parts):
        send_half(parts, 4)
        send_half(parts, 0)

    def answer():
        @pl.when(upper)
        def _():
            lax.fori_loop(NEAR, PEERS, greet, 0)

    def turn(j):
        keys_t[j] = full[K, j].T

    for a in range(4):
        in_copy(a, 0).wait_recv()
    corr_copy(0).wait_recv()

    @pl.when(place < 2)
    def _():
        first = set()
        for i in (0, 1):
            turn(i)
            rows(i, first)
        send((0, 1, 0))
        for a in (K, Q, G, V):
            for r in (1, 2):
                in_copy(a, r).wait_recv()
        for r in (1, 2):
            corr_copy(r).wait_recv()
        turn(2)
        turn(3)
        rows(3, first)
        rows(2, first)
        for j in range(SPAN):
            finish(j)
        send((0, 3, 2), (1, 3, 0))

    @pl.when(place >= 2)
    def _():
        first = set()
        turn(2)
        turn(3)
        for a in (K, V):
            for r in (1, 2):
                in_copy(a, r).wait_recv()
        turn(0)
        turn(1)
        rows(2, first)
        rows(3, first)
        finish(2)
        finish(3)
        send((0, 3, 2))
        for a in (Q, G):
            for r in (1, 2):
                in_copy(a, r).wait_recv()
        for r in (1, 2):
            corr_copy(r).wait_recv()
        rows(1, first)
        rows(0, first)
        finish(0)
        finish(1)
        send((0, 3, 0))

    for a in range(4):
        for r in range(3):
            in_copy(a, r).wait_send()
    for r in range(3):
        corr_copy(r).wait_send()
    own_copy(0, 3).wait()

    def wait(m, carry):
        out_copy(0, 3, (place + m) % SPAN, m // SPAN).wait()
        return carry

    lax.fori_loop(1, PEERS, wait, 0)


def arrange(landed_hbm, dq_out, dk_out, dv_out, landed, wide, done, in_sem, sem):
    loads = [
        pltpu.make_async_copy(landed_hbm.at[a], landed.at[a], in_sem.at[a]) for a in range(3)
    ]
    for load in loads:
        load.start()
    copies = []
    for a, out in enumerate((dq_out, dk_out, dv_out)):
        loads[a].wait()
        wide[a] = landed[a].reshape(HEADS * ROWS, HD).astype(F32)
        for t in range(ROWS):
            done[a, t] = wide[a, pl.ds(t, HEADS, ROWS), :].astype(BF16)
        copies.append(pltpu.make_async_copy(done.at[a], out, sem.at[a]))
        copies[-1].start()
    for copy in copies:
        copy.wait()


def body(q, k, v, o, g):
    flat = [z.reshape(TOK * HL, HD) for z in (k, q, g, v, o)]
    hbm = pl.BlockSpec(memory_space=pltpu.HBM)
    landed = pl.pallas_call(
        kernel,
        out_shape=jax.ShapeDtypeStruct((3, HEADS, ROWS, HD), BF16),
        in_specs=[hbm] * 5,
        out_specs=hbm,
        scratch_shapes=[
            pltpu.VMEM((5, TOK * HL, HD), BF16),
            pltpu.VMEM((TOK * HL, HD), F32),
            pltpu.VMEM((4, HL, TOK, HD), BF16),
            pltpu.VMEM((HL, 8, TOK), F32),
            pltpu.VMEM((HL, TOK, HD), BF16),
            pltpu.VMEM((4, SPAN, TOK, HD), BF16),
            pltpu.VMEM((SPAN, HD, TOK), BF16),
            pltpu.VMEM((SPAN, 8, TOK), F32),
            pltpu.VMEM((2, SPAN, TOK, HD), F32),
            pltpu.VMEM((3, SPAN, TOK, HD), BF16),
            pltpu.SemaphoreType.DMA((5,)),
            pltpu.SemaphoreType.DMA((4, 3)),
            pltpu.SemaphoreType.DMA((4, 3)),
            pltpu.SemaphoreType.DMA((3,)),
            pltpu.SemaphoreType.DMA((3,)),
            pltpu.SemaphoreType.DMA((PEERS,)),
            pltpu.SemaphoreType.DMA((PEERS,)),
            pltpu.SemaphoreType.DMA,
        ],
        compiler_params=pltpu.CompilerParams(
            collective_id=0, has_side_effects=True, vmem_limit_bytes=60 * 1024 * 1024
        ),
        name="grads",
    )(*flat)
    return pl.pallas_call(
        arrange,
        out_shape=[jax.ShapeDtypeStruct((ROWS, HEADS, HD), BF16)] * 3,
        in_specs=[hbm],
        out_specs=[hbm] * 3,
        scratch_shapes=[
            pltpu.VMEM((3, HEADS, ROWS, HD), BF16),
            pltpu.VMEM((3, HEADS * ROWS, HD), F32),
            pltpu.VMEM((3, ROWS, HEADS, HD), BF16),
            pltpu.SemaphoreType.DMA((3,)),
            pltpu.SemaphoreType.DMA((3,)),
        ],
        compiler_params=pltpu.CompilerParams(vmem_limit_bytes=60 * 1024 * 1024),
        name="arrange",
    )(landed)


def solution(mesh):
    placed = P("seq", "head", None)
    gathered = P(("seq", "head"), None, None)
    return jax.shard_map(
        body,
        mesh=mesh,
        in_specs=(placed,) * 5,
        out_specs=(gathered,) * 3,
        check_vma=False,
    )
```

```python
import functools

import jax
import jax.numpy as jnp
from jax import lax
from jax.experimental import pallas as pl
from jax.experimental.pallas import tpu as pltpu
from jax.sharding import PartitionSpec as P

MESH = pl.DeviceIdType.MESH
BF16 = jnp.bfloat16
F32 = jnp.float32
SPAN = 4
TOK = 256
HL = 4
HD = 128
HEADS = 32
PEERS = 32
NEAR = 16
ROWS = 32
SCALE = HD**-0.5
K, Q, G, V = range(4)

NT = (((1,), (1,)), ((), ()))


def dot(a, b):
    return jnp.dot(a, b, preferred_element_type=F32)


def dot_nt(a, b):
    return lax.dot_general(a, b, NT, preferred_element_type=F32)


def kernel(
    k_hbm, q_hbm, g_hbm, v_hbm, o_hbm,
    landed,
    stage, wide, send_in, send_corr, local_o, full, keys_t, corr, acc, held_w, held_q, grads,
    hbm_sem, in_send, in_recv, c_send, c_recv, out_send, out_recv, own_sem,
):
    seq = lax.axis_index("seq")
    head = lax.axis_index("head")
    base = (seq // SPAN) * SPAN
    place = seq % SPAN
    mine = head * HL + place

    def shifted(h, d):
        return ((h // 4 + d // 4) % 2) * 4 + (h % 4 + d % 4) % 4

    def back(h, d):
        return ((h // 4 + d // 4) % 2) * 4 + (h % 4 + 4 - d % 4) % 4

    loads = []
    for a, ref in enumerate((k_hbm, q_hbm, g_hbm, v_hbm, o_hbm)):
        loads.append(pltpu.make_async_copy(ref, stage.at[a], hbm_sem.at[a]))
        loads[-1].start()

    barrier = pltpu.get_barrier_semaphore()

    def greet(m, carry):
        to = (base + (place + SPAN - m % SPAN) % SPAN, back(head, m // SPAN))
        pl.semaphore_signal(barrier, inc=1, device_id=to, device_id_type=MESH)
        return carry

    lax.fori_loop(1, NEAR, greet, 0)
    upper = head >= 4

    def split_heads(a, store):
        loads[a].wait()
        wide[...] = stage[a].astype(F32)
        for h in range(HL):
            store(h, wide[pl.ds(h, TOK, HL), :].astype(BF16))

    def store_in(a):
        def store(h, rows):
            send_in[a, h] = rows

        return store

    def store_o(h, rows):
        local_o[h] = rows

    same_chip = place + 1 - 2 * (place % 2)
    others = (same_chip, (place + 2) % SPAN, (same_chip + 2) % SPAN)

    def in_copy(a, r):
        return pltpu.make_async_remote_copy(
            src_ref=send_in.at[a, others[r]],
            dst_ref=full.at[a, place],
            send_sem=in_send.at[a, r],
            recv_sem=in_recv.at[a, r],
            device_id=(base + others[r], head),
            device_id_type=MESH,
        )

    def corr_copy(r):
        return pltpu.make_async_remote_copy(
            src_ref=send_corr.at[others[r]],
            dst_ref=corr.at[place],
            send_sem=c_send.at[r],
            recv_sem=c_recv.at[r],
            device_id=(base + others[r], head),
            device_id_type=MESH,
        )

    split_heads(K, store_in(K))
    @pl.when(upper)
    def _():
        pl.semaphore_wait(barrier, PEERS - 1)

    @pl.when(jnp.logical_not(upper))
    def _():
        pl.semaphore_wait(barrier, NEAR - 1)
        lax.fori_loop(NEAR, PEERS, greet, 0)
    for r in (1, 2, 0):
        in_copy(K, r).start()
    split_heads(V, store_in(V))

    @pl.when(place < 2)
    def _():
        for r in (1, 2, 0):
            in_copy(V, r).start()

    for a in (Q, G):
        split_heads(a, store_in(a))
        for r in (1, 2, 0):
            in_copy(a, r).start()

    @pl.when(place >= 2)
    def _():
        for r in (0, 1, 2):
            in_copy(V, r).start()

    split_heads(4, store_o)
    ones = jnp.ones((8, HD), BF16)
    for h in range(HL):
        prod = send_in[G, h].astype(F32) * local_o[h].astype(F32)
        high = prod.astype(BF16)
        low = (prod - high.astype(F32)).astype(BF16)
        send_corr[h] = dot_nt(ones, high) + dot_nt(ones, low)
    for r in (0, 1, 2):
        corr_copy(r).start()
    for a in range(4):
        full[a, place] = send_in[a, place]
    corr[place] = send_corr[place]

    def add(a, j, term, first):
        if (a, j) in first:
            term = acc[a, j] + term
        acc[a, j] = term
        first.add((a, j))

    def pair(i, j, w, first):
        q = full[Q, i]
        g = full[G, i]
        gw = dot_nt(full[V, j], g)
        ds = (w * (gw - corr[i][0:1, :])).astype(BF16)
        add(0, j, dot(ds, q), first)
        return dot(keys_t[j], ds)

    def rows(i, first, end=SPAN):
        q = full[Q, i]
        g = full[G, i]
        row = lax.broadcasted_iota(jnp.int32, (TOK, TOK), 0)
        col = lax.broadcasted_iota(jnp.int32, (TOK, TOK), 1)
        scores = []
        for j in range(i + 1):
            s = dot_nt(full[K, j], q) * SCALE
            if i == j:
                s = jnp.where(row <= col, s, -jnp.inf)
            scores.append(s)
        top = jnp.max(scores[0], axis=0, keepdims=True)
        for s in scores[1:]:
            top = jnp.maximum(top, jnp.max(s, axis=0, keepdims=True))
        exps = [jnp.exp(s - top) for s in scores]
        total = jnp.sum(exps[0], axis=0, keepdims=True)
        for e in exps[1:]:
            total = total + jnp.sum(e, axis=0, keepdims=True)
        inv = 1.0 / total
        dq_t = jnp.zeros((HD, TOK), F32)
        for j in range(i + 1):
            w = exps[j] * inv
            add(1, j, dot(w.astype(BF16), g), first)
            if j < end:
                dq_t = dq_t + pair(i, j, w, first)
            else:
                held_w[i + j - 4] = w
        if i < end:
            grads[0, i] = (dq_t * SCALE).T.astype(BF16)
        else:
            held_q[i - 2] = dq_t

    def rest(i, first):
        dq_t = held_q[i - 2]
        for j in range(2, i + 1):
            dq_t = dq_t + pair(i, j, held_w[i + j - 4], first)
        grads[0, i] = (dq_t * SCALE).T.astype(BF16)

    def finish(j):
        grads[1, j] = (acc[0, j] * SCALE).astype(BF16)
        grads[2, j] = acc[1, j].astype(BF16)

    def out_copy(a0, a1, p, d):
        to_head = shifted(head, d)
        m = d * SPAN + (p + SPAN - place) % SPAN
        return pltpu.make_async_remote_copy(
            src_ref=grads.at[a0:a1, p, pl.ds(pl.multiple_of(to_head * ROWS, ROWS), ROWS)],
            dst_ref=landed.at[a0:a1, mine],
            send_sem=out_send.at[m],
            recv_sem=out_recv.at[m],
            device_id=(base + p, to_head),
            device_id_type=MESH,
        )

    def own_copy(a0, a1):
        return pltpu.make_async_copy(
            grads.at[a0:a1, place, pl.ds(pl.multiple_of(head * ROWS, ROWS), ROWS)],
            landed.at[a0:a1, mine],
            own_sem,
        )

    def send_half(parts, d0):
        def step(t, carry):
            d = d0 + t // 2
            for a0, a1, p0 in parts:
                p = p0 + t % 2
                me = jnp.logical_and(d == 0, p == place)

                @pl.when(me)
                def _():
                    own_copy(a0, a1).start()

                @pl.when(jnp.logical_not(me))
                def _():
                    out_copy(a0, a1, p, d).start()

            return carry

        lax.fori_loop(0, 8, step, 0)

    def send(*parts):
        @pl.when(upper)
        def _():
            send_half(parts, 4)

        send_half(parts, 0)

    def answer():
        @pl.when(upper)
        def _():
            lax.fori_loop(NEAR, PEERS, greet, 0)

    def turn(j):
        keys_t[j] = full[K, j].T

    for a in range(4):
        in_copy(a, 0).wait_recv()
    corr_copy(0).wait_recv()

    @pl.when(place < 2)
    def _():
        first = set()
        answer()
        for i in (0, 1):
            turn(i)
            rows(i, first)
        send((0, 1, 0))
        for a in (K, Q, G):
            for r in (1, 2):
                in_copy(a, r).wait_recv()
        for r in (1, 2):
            corr_copy(r).wait_recv()
        turn(2)
        turn(3)
        rows(2, first, 2)
        rows(3, first, 2)
        finish(0)
        finish(1)
        send((1, 3, 0))
        for r in (1, 2):
            in_copy(V, r).wait_recv()
        rest(2, first)
        rest(3, first)
        finish(2)
        finish(3)
        send((0, 3, 2))

    @pl.when(place >= 2)
    def _():
        first = set()
        turn(2)
        turn(3)
        for a in (K, V):
            for r in (1, 2):
                in_copy(a, r).wait_recv()
        answer()
        turn(0)
        turn(1)
        rows(2, first)
        rows(3, first)
        finish(2)
        finish(3)
        send((0, 3, 2))
        for a in (Q, G):
            for r in (1, 2):
                in_copy(a, r).wait_recv()
        for r in (1, 2):
            corr_copy(r).wait_recv()
        rows(1, first)
        rows(0, first)
        finish(0)
        finish(1)
        send((0, 3, 0))

    @pl.when(jnp.logical_not(upper))
    def _():
        pl.semaphore_wait(barrier, PEERS - NEAR)
        send_half(((0, 3, 2), (0, 3, 0)), 4)

    for a in range(4):
        for r in range(3):
            in_copy(a, r).wait_send()
    for r in range(3):
        corr_copy(r).wait_send()
    own_copy(0, 3).wait()

    def wait(m, carry):
        out_copy(0, 3, (place + m) % SPAN, m // SPAN).wait()
        return carry

    lax.fori_loop(1, PEERS, wait, 0)


def arrange(landed_hbm, dq_out, dk_out, dv_out, landed, wide, done, in_sem, sem):
    loads = [
        pltpu.make_async_copy(landed_hbm.at[a], landed.at[a], in_sem.at[a]) for a in range(3)
    ]
    for load in loads:
        load.start()
    copies = []
    for a, out in enumerate((dq_out, dk_out, dv_out)):
        loads[a].wait()
        wide[a] = landed[a].reshape(HEADS * ROWS, HD).astype(F32)
        for t in range(ROWS):
            done[a, t] = wide[a, pl.ds(t, HEADS, ROWS), :].astype(BF16)
        copies.append(pltpu.make_async_copy(done.at[a], out, sem.at[a]))
        copies[-1].start()
    for copy in copies:
        copy.wait()


def body(q, k, v, o, g):
    flat = [z.reshape(TOK * HL, HD) for z in (k, q, g, v, o)]
    hbm = pl.BlockSpec(memory_space=pltpu.HBM)
    landed = pl.pallas_call(
        kernel,
        out_shape=jax.ShapeDtypeStruct((3, HEADS, ROWS, HD), BF16),
        in_specs=[hbm] * 5,
        out_specs=hbm,
        scratch_shapes=[
            pltpu.VMEM((5, TOK * HL, HD), BF16),
            pltpu.VMEM((TOK * HL, HD), F32),
            pltpu.VMEM((4, HL, TOK, HD), BF16),
            pltpu.VMEM((HL, 8, TOK), F32),
            pltpu.VMEM((HL, TOK, HD), BF16),
            pltpu.VMEM((4, SPAN, TOK, HD), BF16),
            pltpu.VMEM((SPAN, HD, TOK), BF16),
            pltpu.VMEM((SPAN, 8, TOK), F32),
            pltpu.VMEM((2, SPAN, TOK, HD), F32),
            pltpu.VMEM((3, TOK, TOK), F32),
            pltpu.VMEM((2, HD, TOK), F32),
            pltpu.VMEM((3, SPAN, TOK, HD), BF16),
            pltpu.SemaphoreType.DMA((5,)),
            pltpu.SemaphoreType.DMA((4, 3)),
            pltpu.SemaphoreType.DMA((4, 3)),
            pltpu.SemaphoreType.DMA((3,)),
            pltpu.SemaphoreType.DMA((3,)),
            pltpu.SemaphoreType.DMA((PEERS,)),
            pltpu.SemaphoreType.DMA((PEERS,)),
            pltpu.SemaphoreType.DMA,
        ],
        compiler_params=pltpu.CompilerParams(
            collective_id=0, has_side_effects=True, vmem_limit_bytes=60 * 1024 * 1024
        ),
        name="grads",
    )(*flat)
    return pl.pallas_call(
        arrange,
        out_shape=[jax.ShapeDtypeStruct((ROWS, HEADS, HD), BF16)] * 3,
        in_specs=[hbm],
        out_specs=[hbm] * 3,
        scratch_shapes=[
            pltpu.VMEM((3, HEADS, ROWS, HD), BF16),
            pltpu.VMEM((3, HEADS * ROWS, HD), F32),
            pltpu.VMEM((3, ROWS, HEADS, HD), BF16),
            pltpu.SemaphoreType.DMA((3,)),
            pltpu.SemaphoreType.DMA((3,)),
        ],
        compiler_params=pltpu.CompilerParams(vmem_limit_bytes=60 * 1024 * 1024),
        name="arrange",
    )(landed)


def solution(mesh):
    placed = P("seq", "head", None)
    gathered = P(("seq", "head"), None, None)
    return jax.shard_map(
        body,
        mesh=mesh,
        in_specs=(placed,) * 5,
        out_specs=(gathered,) * 3,
        check_vma=False,
    )
```

```python
import functools

import jax
import jax.numpy as jnp
from jax import lax
from jax.experimental import pallas as pl
from jax.experimental.pallas import tpu as pltpu
from jax.sharding import PartitionSpec as P

MESH = pl.DeviceIdType.MESH
BF16 = jnp.bfloat16
F32 = jnp.float32
SPAN = 4
TOK = 256
CHIP = 2 * TOK
HL = 4
HD = 128
HEADS = 32
PEERS = 32
NEAR = 16
ROWS = 32
SCALE = HD**-0.5
LOG2E = 1.4426950408889634
PIECE = 16
K, Q, G, V = range(4)

NT = (((1,), (1,)), ((), ()))


def dot(a, b):
    return jnp.dot(a, b, preferred_element_type=F32)


def dot_nt(a, b):
    return lax.dot_general(a, b, NT, preferred_element_type=F32)


def kernel(
    k_hbm, q_hbm, g_hbm, v_hbm, o_hbm,
    landed,
    stage, wide, send_in, send_corr, local_o, full, keys_t, corr, acc, held_w, held_q, grads,
    hbm_sem, in_send, in_recv, c_send, c_recv, out_send, out_recv, own_sem,
):
    seq = lax.axis_index("seq")
    head = lax.axis_index("head")
    base = (seq // SPAN) * SPAN
    place = seq % SPAN
    mine = head * HL + place

    def shifted(h, d):
        return ((h // 4 + d // 4) % 2) * 4 + (h % 4 + d % 4) % 4

    def back(h, d):
        return ((h // 4 + d // 4) % 2) * 4 + (h % 4 + 4 - d % 4) % 4

    loads = []
    for a, ref in enumerate((k_hbm, q_hbm, g_hbm, v_hbm, o_hbm)):
        loads.append(pltpu.make_async_copy(ref, stage.at[a], hbm_sem.at[a]))
        loads[-1].start()

    barrier = pltpu.get_barrier_semaphore()

    def greet(m, carry):
        to = (base + (place + SPAN - m % SPAN) % SPAN, back(head, m // SPAN))
        pl.semaphore_signal(barrier, inc=1, device_id=to, device_id_type=MESH)
        return carry

    lax.fori_loop(1, NEAR, greet, 0)
    upper = head >= 4

    def split_heads(a, store):
        loads[a].wait()
        wide[...] = stage[a].astype(F32)
        for h in range(HL):
            store(h, wide[pl.ds(h, TOK, HL), :].astype(BF16))

    def store_in(a):
        def put(h, rows):
            send_in[a, h] = rows

        return put

    def store_o(h, rows):
        local_o[h] = rows

    same_chip = place + 1 - 2 * (place % 2)
    others = (same_chip, (place + 2) % SPAN, (same_chip + 2) % SPAN)

    def in_copy(a, r):
        return pltpu.make_async_remote_copy(
            src_ref=send_in.at[a, others[r]],
            dst_ref=full.at[a, place],
            send_sem=in_send.at[a, r],
            recv_sem=in_recv.at[a, r],
            device_id=(base + others[r], head),
            device_id_type=MESH,
        )

    def corr_copy(r):
        return pltpu.make_async_remote_copy(
            src_ref=send_corr.at[others[r]],
            dst_ref=corr.at[place],
            send_sem=c_send.at[r],
            recv_sem=c_recv.at[r],
            device_id=(base + others[r], head),
            device_id_type=MESH,
        )

    split_heads(K, store_in(K))
    @pl.when(upper)
    def _():
        pl.semaphore_wait(barrier, PEERS - 1)

    @pl.when(jnp.logical_not(upper))
    def _():
        pl.semaphore_wait(barrier, NEAR - 1)
        lax.fori_loop(NEAR, PEERS, greet, 0)
    for r in (1, 2, 0):
        in_copy(K, r).start()
    split_heads(V, store_in(V))

    @pl.when(place < 2)
    def _():
        for r in (1, 2, 0):
            in_copy(V, r).start()

    for a in (Q, G):
        split_heads(a, store_in(a))
        for r in (1, 2, 0):
            in_copy(a, r).start()

    @pl.when(place >= 2)
    def _():
        for r in (0, 1, 2):
            in_copy(V, r).start()

    split_heads(4, store_o)
    ones = jnp.ones((8, HD), BF16)
    for h in range(HL):
        prod = send_in[G, h].astype(F32) * local_o[h].astype(F32)
        high = prod.astype(BF16)
        low = (prod - high.astype(F32)).astype(BF16)
        send_corr[h] = dot_nt(ones, high) + dot_nt(ones, low)
    for r in (0, 1, 2):
        corr_copy(r).start()
    for a in range(4):
        full[a, place] = send_in[a, place]
    corr[place] = send_corr[place]

    def add(a, j, term, first):
        if (a, j) in first:
            term = acc[a, j] + term
        acc[a, j] = term
        first.add((a, j))

    def part(a, i):
        return full[a, 2 * i : 2 * i + 2].reshape(CHIP, HD)

    def pair(i, j, w, first):
        gw = dot_nt(part(V, j), part(G, i))
        c = jnp.concatenate([corr[2 * i, 0:1], corr[2 * i + 1, 0:1]], axis=1)
        ds = (w * (gw - c)).astype(BF16)
        add(0, j, dot(ds, part(Q, i)), first)
        return dot(keys_t[j], ds)

    def store(a, i, term):
        term = term.astype(BF16).reshape(2, TOK // ROWS, ROWS, HD)
        grads[2 * i : 2 * i + 2, :, a] = term

    def store_dq(i, dq_t):
        store(0, i, (dq_t * SCALE).T)

    def rows(i, first, hold=None):
        q = part(Q, i)
        g = part(G, i)
        row = lax.broadcasted_iota(jnp.int32, (CHIP, CHIP), 0)
        col = lax.broadcasted_iota(jnp.int32, (CHIP, CHIP), 1)
        scores = []
        for j in range(i + 1):
            s = dot_nt(part(K, j), q) * (SCALE * LOG2E)
            if i == j:
                s = jnp.where(row <= col, s, -jnp.inf)
            scores.append(s)
        top = jnp.max(scores[0], axis=0, keepdims=True)
        for s in scores[1:]:
            top = jnp.maximum(top, jnp.max(s, axis=0, keepdims=True))
        exps = [jnp.exp2(s - top) for s in scores]
        total = jnp.sum(exps[0], axis=0, keepdims=True)
        for e in exps[1:]:
            total = total + jnp.sum(e, axis=0, keepdims=True)
        inv = 1.0 / total
        dq_t = jnp.zeros((HD, CHIP), F32)
        for j in range(i + 1):
            w = exps[j] * inv
            if j == hold:
                held_w[...] = w
            else:
                dq_t = dq_t + pair(i, j, w, first)
            if j != hold or j == i:
                add(1, j, dot(w.astype(BF16), g), first)
        if hold is None:
            store_dq(i, dq_t)
        else:
            held_q[...] = dq_t

    def rest(hold, first):
        w = held_w[...]
        store_dq(1, held_q[...] + pair(1, hold, w, first))
        return w

    def finish(j):
        store(1, j, acc[0, j] * SCALE)
        store(2, j, acc[1, j])

    def out_copy(a0, a1, p, d):
        to_head = shifted(head, d)
        m = d * SPAN + (p + SPAN - place) % SPAN
        return pltpu.make_async_remote_copy(
            src_ref=grads.at[p, to_head, a0:a1],
            dst_ref=landed.at[mine, a0:a1],
            send_sem=out_send.at[m],
            recv_sem=out_recv.at[m],
            device_id=(base + p, to_head),
            device_id_type=MESH,
        )

    def own_copy(a0, a1):
        return pltpu.make_async_copy(
            grads.at[place, head, a0:a1],
            landed.at[mine, a0:a1],
            own_sem,
        )

    def send_half(parts, d0):
        def step(t, carry):
            d = d0 + t // 2
            for a0, a1, p0 in parts:
                p = p0 + t % 2
                me = jnp.logical_and(d == 0, p == place)

                @pl.when(me)
                def _():
                    own_copy(a0, a1).start()

                @pl.when(jnp.logical_not(me))
                def _():
                    out_copy(a0, a1, p, d).start()

            return carry

        lax.fori_loop(0, 8, step, 0)

    def send(*parts):
        @pl.when(upper)
        def _():
            send_half(parts, 4)

        send_half(parts, 0)

    def answer():
        @pl.when(upper)
        def _():
            lax.fori_loop(NEAR, PEERS, greet, 0)

    def turn(j):
        keys_t[j] = part(K, j).T

    for a in range(4):
        in_copy(a, 0).wait_recv()
    corr_copy(0).wait_recv()

    @pl.when(place < 2)
    def _():
        first = set()
        answer()
        turn(0)
        rows(0, first)
        send((0, 1, 0))
        for a in (K, Q, G):
            for r in (1, 2):
                in_copy(a, r).wait_recv()
        for r in (1, 2):
            corr_copy(r).wait_recv()
        turn(1)
        rows(1, first, hold=1)
        finish(0)
        send((1, 3, 0))
        for r in (1, 2):
            in_copy(V, r).wait_recv()
        rest(1, first)
        finish(1)
        send((0, 3, 2))

    @pl.when(place >= 2)
    def _():
        first = set()
        turn(1)
        for r in (1, 2):
            in_copy(K, r).wait_recv()
        turn(0)
        rows(1, first, hold=0)
        answer()
        finish(1)
        send((1, 3, 2))
        for r in (1, 2):
            in_copy(V, r).wait_recv()
        w = rest(0, first)
        send((0, 1, 2))
        add(1, 0, dot(w.astype(BF16), part(G, 1)), first)
        for a in (Q, G):
            for r in (1, 2):
                in_copy(a, r).wait_recv()
        for r in (1, 2):
            corr_copy(r).wait_recv()
        rows(0, first)
        finish(0)
        send((0, 3, 0))

    @pl.when(jnp.logical_not(upper))
    def _():
        pl.semaphore_wait(barrier, PEERS - NEAR)
        send_half(((0, 3, 2), (0, 3, 0)), 4)

    for a in range(4):
        for r in range(3):
            in_copy(a, r).wait_send()
    for r in range(3):
        corr_copy(r).wait_send()
    own_copy(0, 3).wait()

    def wait(m, carry):
        out_copy(0, 3, (place + m) % SPAN, m // SPAN).wait()
        return carry

    lax.fori_loop(1, PEERS, wait, 0)


def arrange(landed_hbm, dq_out, dk_out, dv_out, landed, wide, done, in_sem, out_sem):
    pieces = [(a, h) for a in range(3) for h in range(ROWS // PIECE)]

    def load(a, h):
        return pltpu.make_async_copy(
            landed_hbm.at[:, a, pl.ds(h * PIECE, PIECE)], landed.at[a, h], in_sem.at[a, h]
        )

    def store(a, h):
        out = (dq_out, dk_out, dv_out)[a]
        return pltpu.make_async_copy(
            done.at[a, h], out.at[pl.ds(h * PIECE, PIECE)], out_sem.at[a, h]
        )

    for a, h in pieces:
        load(a, h).start()
    for a, h in pieces:
        load(a, h).wait()
        wide[a, h] = landed[a, h].reshape(HEADS * PIECE, HD).astype(F32)
        for t in range(PIECE):
            done[a, h, t] = wide[a, h, pl.ds(t, HEADS, PIECE), :].astype(BF16)
        store(a, h).start()
    for a, h in pieces:
        store(a, h).wait()


def body(q, k, v, o, g):
    flat = [z.reshape(TOK * HL, HD) for z in (k, q, g, v, o)]
    hbm = pl.BlockSpec(memory_space=pltpu.HBM)
    landed = pl.pallas_call(
        kernel,
        out_shape=jax.ShapeDtypeStruct((HEADS, 3, ROWS, HD), BF16),
        in_specs=[hbm] * 5,
        out_specs=hbm,
        scratch_shapes=[
            pltpu.VMEM((5, TOK * HL, HD), BF16),
            pltpu.VMEM((TOK * HL, HD), F32),
            pltpu.VMEM((4, HL, TOK, HD), BF16),
            pltpu.VMEM((HL, 8, TOK), F32),
            pltpu.VMEM((HL, TOK, HD), BF16),
            pltpu.VMEM((4, SPAN, TOK, HD), BF16),
            pltpu.VMEM((2, HD, CHIP), BF16),
            pltpu.VMEM((SPAN, 8, TOK), F32),
            pltpu.VMEM((2, 2, CHIP, HD), F32),
            pltpu.VMEM((CHIP, CHIP), F32),
            pltpu.VMEM((HD, CHIP), F32),
            pltpu.VMEM((SPAN, TOK // ROWS, 3, ROWS, HD), BF16),
            pltpu.SemaphoreType.DMA((5,)),
            pltpu.SemaphoreType.DMA((4, 3)),
            pltpu.SemaphoreType.DMA((4, 3)),
            pltpu.SemaphoreType.DMA((3,)),
            pltpu.SemaphoreType.DMA((3,)),
            pltpu.SemaphoreType.DMA((PEERS,)),
            pltpu.SemaphoreType.DMA((PEERS,)),
            pltpu.SemaphoreType.DMA,
        ],
        compiler_params=pltpu.CompilerParams(
            collective_id=0, has_side_effects=True, vmem_limit_bytes=60 * 1024 * 1024
        ),
        name="grads",
    )(*flat)
    return pl.pallas_call(
        arrange,
        out_shape=[jax.ShapeDtypeStruct((ROWS, HEADS, HD), BF16)] * 3,
        in_specs=[hbm],
        out_specs=[hbm] * 3,
        scratch_shapes=[
            pltpu.VMEM((3, ROWS // PIECE, HEADS, PIECE, HD), BF16),
            pltpu.VMEM((3, ROWS // PIECE, HEADS * PIECE, HD), F32),
            pltpu.VMEM((3, ROWS // PIECE, PIECE, HEADS, HD), BF16),
            pltpu.SemaphoreType.DMA((3, ROWS // PIECE)),
            pltpu.SemaphoreType.DMA((3, ROWS // PIECE)),
        ],
        compiler_params=pltpu.CompilerParams(vmem_limit_bytes=60 * 1024 * 1024),
        name="arrange",
    )(landed)


def solution(mesh):
    placed = P("seq", "head", None)
    gathered = P(("seq", "head"), None, None)
    return jax.shard_map(
        body,
        mesh=mesh,
        in_specs=(placed,) * 5,
        out_specs=(gathered,) * 3,
        check_vma=False,
    )
```

```python
import functools

import jax
import jax.numpy as jnp
from jax import lax
from jax.experimental import pallas as pl
from jax.experimental.pallas import tpu as pltpu
from jax.sharding import PartitionSpec as P

MESH = pl.DeviceIdType.MESH
BF16 = jnp.bfloat16
F32 = jnp.float32
SPAN = 4
TOK = 256
CHIP = 2 * TOK
HL = 4
HD = 128
HEADS = 32
PEERS = 32
NEAR = 16
ROWS = 32
SCALE = HD**-0.5
LOG2E = 1.4426950408889634
PIECE = 16
K, Q, G, V = range(4)

NT = (((1,), (1,)), ((), ()))


def dot(a, b):
    return jnp.dot(a, b, preferred_element_type=F32)


def dot_nt(a, b):
    return lax.dot_general(a, b, NT, preferred_element_type=F32)


def kernel(
    k_hbm, q_hbm, g_hbm, v_hbm, o_hbm,
    landed,
    stage, wide, send_in, send_corr, local_o, full, keys_t, corr, acc, held_w, held_q, grads,
    hbm_sem, in_send, in_recv, c_send, c_recv, out_send, out_recv, own_sem,
):
    seq = lax.axis_index("seq")
    head = lax.axis_index("head")
    base = (seq // SPAN) * SPAN
    place = seq % SPAN
    mine = head * HL + place

    def shifted(h, d):
        return ((h // 4 + d // 4) % 2) * 4 + (h % 4 + d % 4) % 4

    def back(h, d):
        return ((h // 4 + d // 4) % 2) * 4 + (h % 4 + 4 - d % 4) % 4

    loads = []
    for a, ref in enumerate((k_hbm, q_hbm, g_hbm, v_hbm, o_hbm)):
        loads.append(pltpu.make_async_copy(ref, stage.at[a], hbm_sem.at[a]))
        loads[-1].start()

    barrier = pltpu.get_barrier_semaphore()

    def greet(m, carry):
        to = (base + (place + SPAN - m % SPAN) % SPAN, back(head, m // SPAN))
        pl.semaphore_signal(barrier, inc=1, device_id=to, device_id_type=MESH)
        return carry

    lax.fori_loop(1, NEAR, greet, 0)
    upper = head >= 4
    prompt = (seq // SPAN) % 4 == 3

    def split_heads(a, store):
        loads[a].wait()
        wide[...] = stage[a].astype(F32)
        for h in range(HL):
            store(h, wide[pl.ds(h, TOK, HL), :].astype(BF16))

    def store_in(a):
        def put(h, rows):
            send_in[a, h] = rows

        return put

    def store_o(h, rows):
        local_o[h] = rows

    same_chip = place + 1 - 2 * (place % 2)
    others = (same_chip, (place + 2) % SPAN, (same_chip + 2) % SPAN)

    def in_copy(a, r):
        return pltpu.make_async_remote_copy(
            src_ref=send_in.at[a, others[r]],
            dst_ref=full.at[a, place],
            send_sem=in_send.at[a, r],
            recv_sem=in_recv.at[a, r],
            device_id=(base + others[r], head),
            device_id_type=MESH,
        )

    def corr_copy(r):
        return pltpu.make_async_remote_copy(
            src_ref=send_corr.at[others[r]],
            dst_ref=corr.at[place],
            send_sem=c_send.at[r],
            recv_sem=c_recv.at[r],
            device_id=(base + others[r], head),
            device_id_type=MESH,
        )

    split_heads(K, store_in(K))
    @pl.when(upper)
    def _():
        pl.semaphore_wait(barrier, PEERS - 1)

    @pl.when(jnp.logical_and(upper, prompt))
    def _():
        lax.fori_loop(NEAR, PEERS, greet, 0)

    @pl.when(jnp.logical_not(upper))
    def _():
        pl.semaphore_wait(barrier, NEAR - 1)
        lax.fori_loop(NEAR, PEERS, greet, 0)
    for r in (1, 2, 0):
        in_copy(K, r).start()
    split_heads(V, store_in(V))

    @pl.when(place < 2)
    def _():
        for r in (1, 2, 0):
            in_copy(V, r).start()

    for a in (Q, G):
        split_heads(a, store_in(a))
        for r in (1, 2, 0):
            in_copy(a, r).start()

    @pl.when(place >= 2)
    def _():
        for r in (0, 1, 2):
            in_copy(V, r).start()

    split_heads(4, store_o)
    ones = jnp.ones((8, HD), BF16)
    for h in range(HL):
        prod = send_in[G, h].astype(F32) * local_o[h].astype(F32)
        high = prod.astype(BF16)
        low = (prod - high.astype(F32)).astype(BF16)
        send_corr[h] = dot_nt(ones, high) + dot_nt(ones, low)
    for r in (0, 1, 2):
        corr_copy(r).start()
    for a in range(4):
        full[a, place] = send_in[a, place]
    corr[place] = send_corr[place]

    def add(a, j, term, first):
        if (a, j) in first:
            term = acc[a, j] + term
        acc[a, j] = term
        first.add((a, j))

    def part(a, i):
        return full[a, 2 * i : 2 * i + 2].reshape(CHIP, HD)

    def pair(i, j, w, first):
        gw = dot_nt(part(V, j), part(G, i))
        c = jnp.concatenate([corr[2 * i, 0:1], corr[2 * i + 1, 0:1]], axis=1)
        ds = (w * (gw - c)).astype(BF16)
        add(0, j, dot(ds, part(Q, i)), first)
        return dot(keys_t[j], ds)

    def store(a, i, term):
        term = term.astype(BF16).reshape(2, TOK // ROWS, ROWS, HD)
        grads[2 * i : 2 * i + 2, :, a] = term

    def store_dq(i, dq_t):
        store(0, i, (dq_t * SCALE).T)

    def rows(i, first, hold=None):
        q = part(Q, i)
        g = part(G, i)
        row = lax.broadcasted_iota(jnp.int32, (CHIP, CHIP), 0)
        col = lax.broadcasted_iota(jnp.int32, (CHIP, CHIP), 1)
        scores = []
        for j in range(i + 1):
            s = dot_nt(part(K, j), q) * (SCALE * LOG2E)
            if i == j:
                s = jnp.where(row <= col, s, -jnp.inf)
            scores.append(s)
        top = jnp.max(scores[0], axis=0, keepdims=True)
        for s in scores[1:]:
            top = jnp.maximum(top, jnp.max(s, axis=0, keepdims=True))
        exps = [jnp.exp2(s - top) for s in scores]
        total = jnp.sum(exps[0], axis=0, keepdims=True)
        for e in exps[1:]:
            total = total + jnp.sum(e, axis=0, keepdims=True)
        inv = 1.0 / total
        dq_t = jnp.zeros((HD, CHIP), F32)
        for j in range(i + 1):
            w = exps[j] * inv
            if j == hold:
                held_w[...] = w
            else:
                dq_t = dq_t + pair(i, j, w, first)
            if j != hold or j == i:
                add(1, j, dot(w.astype(BF16), g), first)
        if hold is None:
            store_dq(i, dq_t)
        else:
            held_q[...] = dq_t

    def rest(hold, first):
        w = held_w[...]
        store_dq(1, held_q[...] + pair(1, hold, w, first))
        return w

    def finish(j):
        store(1, j, acc[0, j] * SCALE)
        store(2, j, acc[1, j])

    def out_copy(a0, a1, p, d):
        to_head = shifted(head, d)
        m = d * SPAN + (p + SPAN - place) % SPAN
        return pltpu.make_async_remote_copy(
            src_ref=grads.at[p, to_head, a0:a1],
            dst_ref=landed.at[mine, a0:a1],
            send_sem=out_send.at[m],
            recv_sem=out_recv.at[m],
            device_id=(base + p, to_head),
            device_id_type=MESH,
        )

    def own_copy(a0, a1):
        return pltpu.make_async_copy(
            grads.at[place, head, a0:a1],
            landed.at[mine, a0:a1],
            own_sem,
        )

    def send_half(parts, d0):
        def step(t, carry):
            d = d0 + t // 2
            for a0, a1, p0 in parts:
                p = p0 + t % 2
                me = jnp.logical_and(d == 0, p == place)

                @pl.when(me)
                def _():
                    own_copy(a0, a1).start()

                @pl.when(jnp.logical_not(me))
                def _():
                    out_copy(a0, a1, p, d).start()

            return carry

        lax.fori_loop(0, 8, step, 0)

    def send(*parts):
        @pl.when(upper)
        def _():
            send_half(parts, 4)

        send_half(parts, 0)

    def answer():
        @pl.when(jnp.logical_and(upper, jnp.logical_not(prompt)))
        def _():
            lax.fori_loop(NEAR, PEERS, greet, 0)

    def turn(j):
        keys_t[j] = part(K, j).T

    for a in range(4):
        in_copy(a, 0).wait_recv()
    corr_copy(0).wait_recv()

    @pl.when(place < 2)
    def _():
        first = set()
        answer()
        turn(0)
        rows(0, first)
        send((0, 1, 0))
        for a in (K, Q, G):
            for r in (1, 2):
                in_copy(a, r).wait_recv()
        for r in (1, 2):
            corr_copy(r).wait_recv()
        turn(1)
        rows(1, first, hold=1)
        finish(0)
        send((1, 3, 0))
        for r in (1, 2):
            in_copy(V, r).wait_recv()
        rest(1, first)
        finish(1)
        send((0, 3, 2))

    @pl.when(place >= 2)
    def _():
        first = set()
        turn(1)
        for r in (1, 2):
            in_copy(K, r).wait_recv()
        turn(0)
        rows(1, first, hold=0)
        answer()
        finish(1)
        send((1, 3, 2))
        for r in (1, 2):
            in_copy(V, r).wait_recv()
        w = rest(0, first)
        send((0, 1, 2))
        add(1, 0, dot(w.astype(BF16), part(G, 1)), first)
        for a in (Q, G):
            for r in (1, 2):
                in_copy(a, r).wait_recv()
        for r in (1, 2):
            corr_copy(r).wait_recv()
        rows(0, first)
        finish(0)
        send((0, 3, 0))

    @pl.when(jnp.logical_not(upper))
    def _():
        pl.semaphore_wait(barrier, PEERS - NEAR)
        send_half(((0, 3, 2), (0, 3, 0)), 4)

    for a in range(4):
        for r in range(3):
            in_copy(a, r).wait_send()
    for r in range(3):
        corr_copy(r).wait_send()
    own_copy(0, 3).wait()

    def wait(m, carry):
        out_copy(0, 3, (place + m) % SPAN, m // SPAN).wait()
        return carry

    lax.fori_loop(1, PEERS, wait, 0)


def arrange(landed_hbm, dq_out, dk_out, dv_out, landed, wide, done, in_sem, out_sem):
    pieces = [(a, h) for a in range(3) for h in range(ROWS // PIECE)]

    def load(a, h):
        return pltpu.make_async_copy(
            landed_hbm.at[:, a, pl.ds(h * PIECE, PIECE)], landed.at[a, h], in_sem.at[a, h]
        )

    def store(a, h):
        out = (dq_out, dk_out, dv_out)[a]
        return pltpu.make_async_copy(
            done.at[a, h], out.at[pl.ds(h * PIECE, PIECE)], out_sem.at[a, h]
        )

    for a, h in pieces:
        load(a, h).start()
    for a, h in pieces:
        load(a, h).wait()
        wide[a, h] = landed[a, h].reshape(HEADS * PIECE, HD).astype(F32)
        for t in range(PIECE):
            done[a, h, t] = wide[a, h, pl.ds(t, HEADS, PIECE), :].astype(BF16)
        store(a, h).start()
    for a, h in pieces:
        store(a, h).wait()


def body(q, k, v, o, g):
    flat = [z.reshape(TOK * HL, HD) for z in (k, q, g, v, o)]
    hbm = pl.BlockSpec(memory_space=pltpu.HBM)
    landed = pl.pallas_call(
        kernel,
        out_shape=jax.ShapeDtypeStruct((HEADS, 3, ROWS, HD), BF16),
        in_specs=[hbm] * 5,
        out_specs=hbm,
        scratch_shapes=[
            pltpu.VMEM((5, TOK * HL, HD), BF16),
            pltpu.VMEM((TOK * HL, HD), F32),
            pltpu.VMEM((4, HL, TOK, HD), BF16),
            pltpu.VMEM((HL, 8, TOK), F32),
            pltpu.VMEM((HL, TOK, HD), BF16),
            pltpu.VMEM((4, SPAN, TOK, HD), BF16),
            pltpu.VMEM((2, HD, CHIP), BF16),
            pltpu.VMEM((SPAN, 8, TOK), F32),
            pltpu.VMEM((2, 2, CHIP, HD), F32),
            pltpu.VMEM((CHIP, CHIP), F32),
            pltpu.VMEM((HD, CHIP), F32),
            pltpu.VMEM((SPAN, TOK // ROWS, 3, ROWS, HD), BF16),
            pltpu.SemaphoreType.DMA((5,)),
            pltpu.SemaphoreType.DMA((4, 3)),
            pltpu.SemaphoreType.DMA((4, 3)),
            pltpu.SemaphoreType.DMA((3,)),
            pltpu.SemaphoreType.DMA((3,)),
            pltpu.SemaphoreType.DMA((PEERS,)),
            pltpu.SemaphoreType.DMA((PEERS,)),
            pltpu.SemaphoreType.DMA,
        ],
        compiler_params=pltpu.CompilerParams(
            collective_id=0, has_side_effects=True, vmem_limit_bytes=60 * 1024 * 1024
        ),
        name="grads",
    )(*flat)
    return pl.pallas_call(
        arrange,
        out_shape=[jax.ShapeDtypeStruct((ROWS, HEADS, HD), BF16)] * 3,
        in_specs=[hbm],
        out_specs=[hbm] * 3,
        scratch_shapes=[
            pltpu.VMEM((3, ROWS // PIECE, HEADS, PIECE, HD), BF16),
            pltpu.VMEM((3, ROWS // PIECE, HEADS * PIECE, HD), F32),
            pltpu.VMEM((3, ROWS // PIECE, PIECE, HEADS, HD), BF16),
            pltpu.SemaphoreType.DMA((3, ROWS // PIECE)),
            pltpu.SemaphoreType.DMA((3, ROWS // PIECE)),
        ],
        compiler_params=pltpu.CompilerParams(vmem_limit_bytes=60 * 1024 * 1024),
        name="arrange",
    )(landed)


def solution(mesh):
    placed = P("seq", "head", None)
    gathered = P(("seq", "head"), None, None)
    return jax.shard_map(
        body,
        mesh=mesh,
        in_specs=(placed,) * 5,
        out_specs=(gathered,) * 3,
        check_vma=False,
    )
```
